256 devices in a mesh: space: 64 (over z_lo, y, x, core), chan: 4 (over z_hi).
Axes of the slice: x: 4, y: 4, z: 8 (z_hi: 4, z_lo: 2; z = z_hi * 2 + z_lo), core: 2. Of those that a mesh axis runs over, the one named last changes fastest.
Arguments:
- volume: bfloat16 [256, 128, 16, 64], P(None, 'space', 'chan'), may hold values from -6 to 6
- first_filter: bfloat16 [27, 256, 256], replicated, may hold values from -0.078125 to 0.078125
- first_bias: float32 [256], replicated, may hold values from -3 to 3
- second_filter: bfloat16 [27, 256, 256], replicated, may hold values from -0.078125 to 0.078125
- second_bias: float32 [256], replicated, may hold values from -3 to 3
Outputs:
- features: bfloat16 [256, 128, 16, 64], P('chan', 'space')
The draws below stay inside these ranges and needn't reach their ends.
All inputs are finite; a program needn't handle non-finite values.
Results may differ from the reference program's by a relative error of at most 0.0044.
Values may be sent and summed in bfloat16 or wider, within the bound.
A program may use at most 192 MiB of HBM per device.

```python
import jax
import jax.numpy as jnp
from jax import lax

C = 256
Y = 16
Z = 64
TAPS = 27
X = 128


def level_of(rng, dims, shards, smallest, largest):
    level, own = 1.0, jax.random.fold_in(rng, 6)
    for dim, blocks in shards:
        heights = jnp.exp(jax.random.uniform(jax.random.fold_in(own, dim), (blocks,), jnp.float32, smallest / len(shards), largest / len(shards)))
        level = level * jnp.repeat(heights, dims[dim] // blocks).reshape([-1 if axis == dim else 1 for axis in range(len(dims))])
    return level


def normal_values(rng, shape, deviation, limit, split=(), kind=jnp.bfloat16):
    values = jax.random.normal(rng, shape, jnp.float32) * deviation
    if len(split) > 0:
        values = level_of(rng, shape, split, -0.22, 0.18) * values
    return jnp.clip(values, min=-limit, max=limit).astype(kind)


def setup_inputs(seed: int = 0) -> dict:
    splits = jax.random.split(jax.random.key(seed), 6)
    volume = normal_values(splits[0], (C, X, Y, Z), 1.0, 6.0, ((1, 64), (2, 4)))
    first_filter = normal_values(splits[1], (TAPS, C, C), (TAPS * C) ** -0.5, 0.078125)
    first_bias = normal_values(splits[2], (C,), 0.5, 3.0, (), jnp.float32)
    second_filter = normal_values(splits[3], (TAPS, C, C), (TAPS * C) ** -0.5, 0.078125)
    second_bias = normal_values(splits[4], (C,), 0.5, 3.0, (), jnp.float32)
    return dict(volume=volume, first_filter=first_filter, first_bias=first_bias, second_filter=second_filter, second_bias=second_bias)


def leaky(value):
    return jnp.where(value >= 0.0, value, 0.3 * value)


def convolve(activation, filters):
    kernel = filters.astype(jnp.float32).reshape(3, 3, 3, C, C)
    kernel = jnp.transpose(kernel, (3, 4, 0, 1, 2))
    result = lax.conv_general_dilated(activation.astype(jnp.float32)[None], kernel, (1, 1, 1), "SAME", dimension_numbers=("NCDHW", "OIDHW", "NCDHW"), precision=lax.Precision.HIGHEST)
    return result[0]


def reference(volume, first_filter, first_bias, second_filter, second_bias):
    hidden = leaky(convolve(volume, first_filter) + first_bias[:, None, None, None]).astype(jnp.bfloat16)
    return leaky(convolve(hidden, second_filter) + second_bias[:, None, None, None]).astype(jnp.bfloat16)
```

```python
import jax
import jax.numpy as jnp
from jax import lax
from jax.experimental import pallas as pl
from jax.experimental.pallas import tpu as pltpu
from jax.sharding import PartitionSpec as P

MESH = pl.DeviceIdType.MESH
F32, BF16 = jnp.float32, jnp.bfloat16
CHAN = 4
SLAB = 64


def leaky(value):
    return jnp.where(value >= 0.0, value, 0.3 * value)


def nt(a, b):
    return lax.dot_general(a, b, (((1,), (1,)), ((), ())), preferred_element_type=F32)


def window(padded, a, b, inner):
    if inner:
        return padded[a : a + 2, 1 + b : 3 + b].reshape(256, 256)
    rows = [padded[a + p, 3 * r + b] for p in range(2) for r in range(2)]
    return jnp.concatenate(rows, axis=0)


def shifted_rows(low, mid, high):
    rows = low.shape[0]
    z = lax.broadcasted_iota(jnp.int32, low.shape, 0) % 64
    up = jnp.where(z == 0, 0.0, pltpu.roll(low, 1, 0))
    down = jnp.where(z == 63, 0.0, pltpu.roll(high, rows - 1, 0))
    return mid + up + down


def shifted_lanes(low, mid, high):
    parts = []
    for first in range(0, low.shape[1], 128):
        cut = slice(first, first + 128)
        z = lax.broadcasted_iota(jnp.int32, (low.shape[0], 128), 1) % 64
        up = jnp.where(z == 0, 0.0, pltpu.roll(low[:, cut], 1, 1))
        down = jnp.where(z == 63, 0.0, pltpu.roll(high[:, cut], 127, 1))
        parts.append(mid[:, cut] + up + down)
    return jnp.concatenate(parts, axis=1)


def accumulate(padded, filters, inner, channels_first):
    sums = [None] * 3
    for a in range(3):
        for b in range(3):
            voxels = window(padded, a, b, inner)
            for c in range(3):
                taps = filters[9 * a + 3 * b + c]
                term = nt(taps, voxels) if channels_first else nt(voxels, taps)
                sums[c] = term if sums[c] is None else sums[c] + term
    return sums


def kernel(
    vol, f1, b1, f2, b2, out,
    one, two, w1, w2, mine, got, rows, local, xs, xr, ys, yr, cs, cr, ts, tr,
):
    s, j = lax.axis_index("space"), lax.axis_index("chan")
    last = lax.axis_size("space") - 1
    has_lo, has_hi = s > 0, s < last
    has_up, has_down = j > 0, j < CHAN - 1

    load_vol = pltpu.make_async_copy(vol, one.at[1:3, 1:5], local.at[0])
    load_f1 = pltpu.make_async_copy(f1, w1, local.at[1])
    load_f2 = pltpu.make_async_copy(f2, w2, local.at[2])
    load_vol.start()
    load_f1.start()
    load_f2.start()

    for block in (one, two):
        for absent, place in (
            (s == 0, (0,)),
            (s == last, (3,)),
            (j == 0, (slice(None), 0)),
            (j == CHAN - 1, (slice(None), 5)),
        ):
            @pl.when(absent)
            def _(block=block, place=place):
                block[place] = jnp.zeros(block.at[place].shape, BF16)

    barrier = pltpu.get_barrier_semaphore()
    for step in range(1, CHAN):
        pl.semaphore_signal(barrier, inc=1, device_id=(s, (j + step) % CHAN), device_id_type=MESH)
    for there, who in ((has_lo, s - 1), (has_hi, s + 1)):
        @pl.when(there)
        def _(who=who):
            pl.semaphore_signal(barrier, inc=1, device_id=(who, j), device_id_type=MESH)
    pl.semaphore_wait(barrier, CHAN - 1 + has_lo.astype(jnp.int32) + has_hi.astype(jnp.int32))

    def remote(src, dst, send, recv, to):
        return pltpu.make_async_remote_copy(
            src_ref=src, dst_ref=dst, send_sem=send, recv_sem=recv, device_id=to, device_id_type=MESH
        )

    def x_copies(n, block, low_src, high_src):
        return (
            (has_lo, has_hi, remote(low_src, block.at[3, 1:5], xs.at[n, 0], xr.at[n, 0], (s - 1, j))),
            (has_hi, has_lo, remote(high_src, block.at[0, 1:5], xs.at[n, 1], xr.at[n, 1], (s + 1, j))),
        )

    def y_copies(n, block, up_src, down_src):
        return (
            (has_up, has_down, remote(up_src, block.at[1:3, 5], ys.at[n, 0], yr.at[n, 0], (s, j - 1))),
            (has_down, has_up, remote(down_src, block.at[1:3, 0], ys.at[n, 1], yr.at[n, 1], (s, j + 1))),
        )

    def corner_copies(n, block):
        copies = []
        for r, (row, there) in enumerate(((0, has_up), (5, has_down))):
            copies.append((
                has_lo & there, has_hi & there,
                remote(block.at[1, row], block.at[3, row], cs.at[n, r, 0], cr.at[n, r, 0], (s - 1, j)),
            ))
            copies.append((
                has_hi & there, has_lo & there,
                remote(block.at[2, row], block.at[0, row], cs.at[n, r, 1], cr.at[n, r, 1], (s + 1, j)),
            ))
        return copies

    def start(copies):
        for sends, _, copy in copies:
            pl.when(sends)(copy.start)

    def arrived(copies):
        for _, receives, copy in copies:
            pl.when(receives)(copy.wait_recv)

    def left(copies):
        for sends, _, copy in copies:
            pl.when(sends)(copy.wait_send)

    y1 = y_copies(0, one, vol.at[:, 0], vol.at[:, 3])
    x1 = x_copies(0, one, vol.at[0], vol.at[1])
    c1 = corner_copies(0, one)
    start(y1)
    start(x1)
    load_vol.wait()
    load_f1.wait()
    arrived(y1)
    start(c1)
    arrived(x1)

    bias1 = b1[...]
    inner = leaky(shifted_rows(*accumulate(one, w1, True, False)) + bias1).astype(BF16)
    two[1:3, 2:4] = inner.reshape(2, 2, 64, 256)
    arrived(c1)
    outer = leaky(shifted_rows(*accumulate(one, w1, False, False)) + bias1).astype(BF16)
    outer = outer.reshape(2, 2, 64, 256)
    two[1:3, 1] = outer[:, 0]
    two[1:3, 4] = outer[:, 1]

    y2 = y_copies(1, two, two.at[1:3, 1], two.at[1:3, 4])
    x2 = x_copies(1, two, two.at[1, 1:5], two.at[2, 1:5])
    c2 = corner_copies(1, two)
    start(y2)
    start(x2)
    load_f2.wait()
    bias2 = jnp.transpose(jnp.broadcast_to(b2[...], (8, 256)))[:, :1]

    def turn(n):
        copies = []
        for step in (2, 1, 3):
            to = (j + step) % CHAN
            copies.append(remote(
                mine.at[n, pl.ds(pl.multiple_of(to * SLAB, SLAB), SLAB)], got.at[n, j],
                ts.at[n, step - 1], tr.at[n, step - 1], (s, to),
            ))
        return copies

    arrived(x2)
    arrived(y2)
    start(c2)
    sent = [turn(0), turn(1)]
    for n in range(2):
        if n == 1:
            arrived(c2)
        block = leaky(shifted_lanes(*accumulate(two, w2, n == 0, True)) + bias2).astype(BF16)
        mine[n] = block
        for copy in sent[n]:
            copy.start()
        got[n, j] = mine[n, pl.ds(pl.multiple_of(j * SLAB, SLAB), SLAB)]
    for copy in sent[0] + sent[1]:
        copy.wait_recv()

    for n in range(2):
        for source in range(CHAN):
            slab = got[n, source].astype(F32)
            low, high = (1, 2) if n == 0 else (0, 3)
            for p in range(2):
                pair = slab[:, 128 * p : 128 * p + 128]
                rows[p, pl.ds((4 * source + low) * SLAB, SLAB)] = pair
                rows[p, pl.ds((4 * source + high) * SLAB, SLAB)] = pltpu.roll(pair, 64, 1)
    for o in range(SLAB):
        for p in range(2):
            out[o, p] = rows[p, pl.ds(o, 16, stride=SLAB), :][:, :64].astype(BF16)

    left(y1)
    left(x1)
    left(c1)
    left(y2)
    left(x2)
    left(c2)
    for copy in sent[0] + sent[1]:
        copy.wait_send()


def on_device(volume, first_filter, first_bias, second_filter, second_bias):
    voxels = jnp.transpose(volume, (1, 2, 3, 0))
    hbm, vmem = pl.BlockSpec(memory_space=pltpu.HBM), pl.BlockSpec(memory_space=pltpu.VMEM)
    dma = pltpu.SemaphoreType.DMA
    return pl.pallas_call(
        kernel,
        out_shape=jax.ShapeDtypeStruct((64, 2, 16, 64), BF16),
        in_specs=[hbm, hbm, vmem, hbm, vmem],
        out_specs=vmem,
        scratch_shapes=[
            pltpu.VMEM((4, 6, 64, 256), BF16),
            pltpu.VMEM((4, 6, 64, 256), BF16),
            pltpu.VMEM((27, 256, 256), BF16),
            pltpu.VMEM((27, 256, 256), BF16),
            pltpu.VMEM((2, 256, 256), BF16),
            pltpu.VMEM((2, CHAN, SLAB, 256), BF16),
            pltpu.VMEM((2, 16 * SLAB, 128), F32),
            dma((3,)),
            dma((2, 2)),
            dma((2, 2)),
            dma((2, 2)),
            dma((2, 2)),
            dma((2, 2, 2)),
            dma((2, 2, 2)),
            dma((2, 3)),
            dma((2, 3)),
        ],
        compiler_params=pltpu.CompilerParams(
            collective_id=0, has_side_effects=True, vmem_limit_bytes=40 * 2**20
        ),
        cost_estimate=pl.CostEstimate(flops=3_623_878_656, bytes_accessed=8_000_000, transcendentals=0),
    )(voxels, first_filter, first_bias.reshape(1, 256), second_filter, second_bias.reshape(1, 256))


def solution(mesh):
    in_specs = (P(None, "space", "chan", None), P(), P(), P(), P())
    out_specs = P("chan", "space", None, None)
    return jax.shard_map(
        on_device, mesh=mesh, in_specs=in_specs, out_specs=out_specs, check_vma=False
    )
```

```python
import jax
import jax.numpy as jnp
from jax import lax
from jax.experimental import pallas as pl
from jax.experimental.pallas import tpu as pltpu
from jax.sharding import PartitionSpec as P

MESH = pl.DeviceIdType.MESH
F32, BF16 = jnp.float32, jnp.bfloat16
CHAN = 4
SLAB = 64
E2, E1, O0, O1, I1 = range(-2, 3)
PLANE_ONE = {E1: 0, E2: 1, O0: 2, O1: 3, I1: 4}
ROW_ONE = {0: 0, 1: 1, 2: 2, 3: 3, -1: 4, 4: 5, -2: 6, 5: 7}
PLANE_TWO = {E1: 0, O0: 1, O1: 2, I1: 3}
ROW_TWO = {0: 0, 1: 1, 2: 2, 3: 3, -1: 4, 4: 5}


def leaky(value):
    return jnp.where(value >= 0.0, value, 0.3 * value)


def nt(a, b):
    return lax.dot_general(a, b, (((1,), (1,)), ((), ())), preferred_element_type=F32)


def shifted_rows(low, mid, high):
    rows = low.shape[0]
    z = lax.broadcasted_iota(jnp.int32, low.shape, 0) % 64
    up = jnp.where(z == 0, 0.0, pltpu.roll(low, 1, 0))
    down = jnp.where(z == 63, 0.0, pltpu.roll(high, rows - 1, 0))
    return mid + up + down


def shifted_lanes(low, mid, high):
    parts = []
    for first in range(0, low.shape[1], 128):
        cut = slice(first, first + 128)
        z = lax.broadcasted_iota(jnp.int32, (low.shape[0], 128), 1) % 64
        up = jnp.where(z == 0, 0.0, pltpu.roll(low[:, cut], 1, 1))
        down = jnp.where(z == 63, 0.0, pltpu.roll(high[:, cut], 127, 1))
        parts.append(mid[:, cut] + up + down)
    return jnp.concatenate(parts, axis=1)


def accumulate(block, plane_of, row_of, planes, rows, filters, channels_first):
    sums = [None] * 3
    for a in range(3):
        for b in range(3):
            pieces = [block[plane_of[p + a - 1], row_of[y + b - 1]] for p in planes for y in rows]
            voxels = jnp.concatenate(pieces, axis=0)
            for c in range(3):
                taps = filters[9 * a + 3 * b + c]
                term = nt(taps, voxels) if channels_first else nt(voxels, taps)
                sums[c] = term if sums[c] is None else sums[c] + term
    return sums


def kernel(
    vol, f1, b1, f2, b2, out,
    one, two, w1, w2, bias, mine, got, rows, local, send_sems, recv_sems, relay,
):
    s, j = lax.axis_index("space"), lax.axis_index("chan")
    flip = s % 2
    sib, ext = s + 1 - 2 * flip, s - 1 + 2 * flip
    has_ext = (ext >= 0) & (ext < lax.axis_size("space"))
    has_up, has_down = j > 0, j < CHAN - 1
    here = (s, j)

    loads = [
        pltpu.make_async_copy(vol.at[flip], one.at[2, 0:4], local.at[0]),
        pltpu.make_async_copy(vol.at[1 - flip], one.at[3, 0:4], local.at[1]),
    ]
    for n, (src, dst) in enumerate(((f1, w1), (f2, w2))):
        for a in range(3):
            first = 9 * (a + flip * (2 - 2 * a))
            loads.append(pltpu.make_async_copy(src.at[pl.ds(first, 9)], dst.at[9 * a : 9 * a + 9], local.at[2 + 3 * n + a]))
    loads.append(pltpu.make_async_copy(b1, bias.at[0], local.at[8]))
    loads.append(pltpu.make_async_copy(b2, bias.at[1], local.at[9]))
    for load in loads[:2]:
        load.start()

    barrier = pltpu.get_barrier_semaphore()
    pl.semaphore_signal(barrier, inc=1, device_id=(sib, j), device_id_type=MESH)
    for there, who in ((has_ext, (ext, j)), (has_up, (s, j - 1)), (has_down, (s, j + 1))):
        @pl.when(there)
        def _(who=who):
            pl.semaphore_signal(barrier, inc=1, device_id=who, device_id_type=MESH)
    for load in loads[2:]:
        load.start()

    def clear(ref, place):
        ref[place] = jnp.zeros(ref.at[place].shape, BF16)

    for block, outer, above, below in ((one, slice(0, 2), (4, 6), (5, 7)), (two, 0, (4,), (5,))):
        pl.when(~has_ext)(lambda block=block, outer=outer: clear(block, (outer,)))
        for there, places in ((has_up, above), (has_down, below)):
            for place in places:
                pl.when(~there)(lambda block=block, place=place: clear(block, (slice(None), place)))

    used = []

    def remote(src, dst, to, sends, receives):
        n = len(used)
        copy = pltpu.make_async_remote_copy(
            src_ref=src, dst_ref=dst, send_sem=send_sems.at[n], recv_sem=recv_sems.at[n],
            device_id=to, device_id_type=MESH,
        )
        used.append((copy, sends, receives))
        return used[-1]

    def start(*copies):
        for copy, sends, _ in copies:
            copy.start() if sends is True else pl.when(sends)(copy.start)

    def arrived(*copies):
        for copy, _, receives in copies:
            copy.wait_recv() if receives is True else pl.when(receives)(copy.wait_recv)

    sibling, outside, above, below = (sib, j), (ext, j), (s, j - 1), (s, j + 1)
    own = slice(0, 4)
    to_sib = remote(one.at[3, own], one.at[4, own], sibling, True, True)
    to_ext = remote(one.at[2:4, own], one.at[0:2, own], outside, has_ext, has_ext)
    near = (
        remote(one.at[2:4, 0], one.at[2:4, ROW_ONE[4]], above, has_up, has_down),
        remote(one.at[2:4, 3], one.at[2:4, ROW_ONE[-1]], below, has_down, has_up),
    )
    far = (
        remote(one.at[2:4, 1], one.at[2:4, ROW_ONE[5]], above, has_up, has_down),
        remote(one.at[2:4, 2], one.at[2:4, ROW_ONE[-2]], below, has_down, has_up),
    )

    def corners(y_up, y_down):
        copies = []
        for y, there in ((y_up, has_up), (y_down, has_down)):
            r = ROW_ONE[y]
            copies.append(remote(one.at[2:4, r], one.at[0:2, r], outside, has_ext & there, has_ext & there))
            copies.append(remote(one.at[3, r], one.at[4, r], sibling, there, there))
        return copies

    near_corners, far_corners = corners(-1, 4), corners(-2, 5)
    inner_two = remote(two.at[2, own], two.at[3, own], sibling, True, True)
    outer_two = remote(two.at[2, 4:6], two.at[3, 4:6], sibling, True, True)
    turns = []
    for n in range(2):
        turns.append([])
        for step in (2, 1, 3):
            to = (j + step) % CHAN
            turns[n].append(remote(
                mine.at[n, pl.ds(pl.multiple_of(to * SLAB, SLAB), SLAB)], got.at[n, j], (s, to), True, True
            ))

    loads[0].wait()
    loads[1].wait()
    pl.semaphore_wait(
        barrier, 1 + has_ext.astype(jnp.int32) + has_up.astype(jnp.int32) + has_down.astype(jnp.int32)
    )
    start(*near, to_ext, to_sib, *far)

    def hidden(y_pair):
        sums = accumulate(one, PLANE_ONE, ROW_ONE, (E1, O0, O1), y_pair, w1, False)
        value = leaky(shifted_rows(*sums) + bias[0]).astype(BF16).reshape(3, 2, 64, 256)
        for i, y in enumerate(y_pair):
            two[0:3, ROW_TWO[y]] = value[:, i]
        pl.when(~has_ext)(lambda: [clear(two, (0, ROW_TWO[y])) for y in y_pair] and None)

    def features(n, y_pair):
        sums = accumulate(two, PLANE_TWO, ROW_TWO, (O0, O1), y_pair, w2, True)
        mine[n] = leaky(shifted_lanes(*sums) + bias2).astype(BF16)
        start(*turns[n])
        got[n, j] = mine[n, pl.ds(pl.multiple_of(j * SLAB, SLAB), SLAB)]

    def regroup(n, y_pair):
        for source in range(CHAN):
            slab = got[n, source].astype(F32)
            for q in range(2):
                pair = slab[:, 128 * q : 128 * q + 128]
                p = q + flip * (1 - 2 * q)
                rows[p, pl.ds((4 * source + y_pair[0]) * SLAB, SLAB)] = pair
                rows[p, pl.ds((4 * source + y_pair[1]) * SLAB, SLAB)] = pltpu.roll(pair, 64, 1)

    arrived(*near)
    start(*near_corners)
    for at, tell in ((1, 0), (2, 3)):
        @pl.when(j == at)
        def _(tell=tell):
            pl.semaphore_signal(relay, inc=1, device_id=(s, tell), device_id_type=MESH)
    for load in loads[2:5] + loads[8:]:
        load.wait()
    arrived(to_ext, to_sib)
    hidden((1, 2))
    arrived(*far)
    start(*far_corners)
    arrived(*near_corners)
    hidden((0, 3))
    start(inner_two)
    arrived(*far_corners)
    hidden((-1, 4))
    for there, r in ((has_up, 4), (has_down, 5)):
        pl.when(~there)(lambda r=r: clear(two, (slice(0, 3), r)))
    start(outer_two)
    for load in loads[5:8]:
        load.wait()
    bias2 = jnp.transpose(jnp.broadcast_to(bias[1], (8, 256)))[:, :1]
    arrived(inner_two)
    pl.when((j == 0) | (j == CHAN - 1))(lambda: pl.semaphore_wait(relay, 1))
    features(0, (1, 2))
    arrived(outer_two)
    features(1, (0, 3))
    arrived(*turns[0])
    regroup(0, (1, 2))
    arrived(*turns[1])
    regroup(1, (0, 3))
    for o in range(SLAB):
        for p in range(2):
            out[o, p] = rows[p, pl.ds(o, 16, stride=SLAB), :][:, :64].astype(BF16)

    for copy, sends, _ in used:
        copy.wait_send() if sends is True else pl.when(sends)(copy.wait_send)


def on_device(volume, first_filter, first_bias, second_filter, second_bias):
    voxels = jnp.transpose(volume, (1, 2, 3, 0))
    hbm, vmem = pl.BlockSpec(memory_space=pltpu.HBM), pl.BlockSpec(memory_space=pltpu.VMEM)
    dma = pltpu.SemaphoreType.DMA
    return pl.pallas_call(
        kernel,
        out_shape=jax.ShapeDtypeStruct((64, 2, 16, 64), BF16),
        in_specs=[hbm] * 5,
        out_specs=vmem,
        scratch_shapes=[
            pltpu.VMEM((5, 8, 64, 256), BF16),
            pltpu.VMEM((4, 6, 64, 256), BF16),
            pltpu.VMEM((27, 256, 256), BF16),
            pltpu.VMEM((27, 256, 256), BF16),
            pltpu.VMEM((2, 1, 256), F32),
            pltpu.VMEM((2, 256, 256), BF16),
            pltpu.VMEM((2, CHAN, SLAB, 256), BF16),
            pltpu.VMEM((2, 16 * SLAB, 128), F32),
            dma((10,)),
            dma((22,)),
            dma((22,)),
            pltpu.SemaphoreType.REGULAR,
        ],
        compiler_params=pltpu.CompilerParams(
            collective_id=0, has_side_effects=True, vmem_limit_bytes=62 * 2**20
        ),
        cost_estimate=pl.CostEstimate(flops=5_900_000_000, bytes_accessed=8_000_000, transcendentals=0),
    )(voxels, first_filter, first_bias.reshape(1, 256), second_filter, second_bias.reshape(1, 256))


def solution(mesh):
    in_specs = (P(None, "space", "chan", None), P(), P(), P(), P())
    out_specs = P("chan", "space", None, None)
    return jax.shard_map(
        on_device, mesh=mesh, in_specs=in_specs, out_specs=out_specs, check_vma=False
    )
```

```python
import jax
import jax.numpy as jnp
from jax import lax
from jax.experimental import pallas as pl
from jax.experimental.pallas import tpu as pltpu
from jax.sharding import PartitionSpec as P

MESH = pl.DeviceIdType.MESH
F32, BF16 = jnp.float32, jnp.bfloat16
CHAN = 4
SLAB = 64
E2, E1, O0, O1, I1 = range(-2, 3)
PLANE_ONE = {E1: 0, E2: 1, O0: 2, O1: 3, I1: 4}
PLANE_TWO = {E1: 0, O0: 1, O1: 2, I1: 3}
FIRST_ONE, FIRST_TWO = -2, -1
OWN_ONE, OWN_TWO = slice(2, 6), slice(1, 5)


def leaky(value):
    return jnp.where(value >= 0.0, value, 0.3 * value)


def nt(a, b):
    return lax.dot_general(a, b, (((1,), (1,)), ((), ())), preferred_element_type=F32)


def shifted_rows(low, mid, high):
    rows = low.shape[0]
    z = lax.broadcasted_iota(jnp.int32, low.shape, 0) % 64
    up = jnp.where(z == 0, 0.0, pltpu.roll(low, 1, 0))
    down = jnp.where(z == 63, 0.0, pltpu.roll(high, rows - 1, 0))
    return mid + up + down


def shifted_lanes(low, mid, high):
    parts = []
    for first in range(0, low.shape[1], 128):
        cut = slice(first, first + 128)
        z = lax.broadcasted_iota(jnp.int32, (low.shape[0], 128), 1) % 64
        up = jnp.where(z == 0, 0.0, pltpu.roll(low[:, cut], 1, 1))
        down = jnp.where(z == 63, 0.0, pltpu.roll(high[:, cut], 127, 1))
        parts.append(mid[:, cut] + up + down)
    return jnp.concatenate(parts, axis=1)


def accumulate(block, plane_of, first_row, planes, step, filters, channels_first):
    sums = [None] * 3
    for a in range(3):
        for b in range(3):
            pieces = [
                block[plane_of[p + a - 1], y + (b - 1 - first_row)] for p in planes for y in (1 - step, 2 + step)
            ]
            voxels = jnp.concatenate(pieces, axis=0)
            for c in range(3):
                taps = filters[9 * a + 3 * b + c]
                term = nt(taps, voxels) if channels_first else nt(voxels, taps)
                sums[c] = term if sums[c] is None else sums[c] + term
    return sums


def kernel(
    vol, f1, b1, f2, b2, got,
    one, two, w1, w2, bias, mine, local, send_sems, recv_sems, relay,
):
    s, j = lax.axis_index("space"), lax.axis_index("chan")
    flip = s % 2
    sib, ext = s + 1 - 2 * flip, s - 1 + 2 * flip
    has_ext = (ext >= 0) & (ext < lax.axis_size("space"))
    has_up, has_down = j > 0, j < CHAN - 1
    half = lax.axis_size("space") // 2
    seam = (s == half - 1) | (s == half)

    loads = [
        pltpu.make_async_copy(vol.at[flip], one.at[2, OWN_ONE], local.at[0]),
        pltpu.make_async_copy(vol.at[1 - flip], one.at[3, OWN_ONE], local.at[1]),
    ]
    for n, (src, dst) in enumerate(((f1, w1), (f2, w2))):
        for a in range(3):
            first = 9 * (a + flip * (2 - 2 * a))
            loads.append(pltpu.make_async_copy(src.at[pl.ds(first, 9)], dst.at[9 * a : 9 * a + 9], local.at[2 + 3 * n + a]))
    loads.append(pltpu.make_async_copy(b1, bias.at[0], local.at[8]))
    loads.append(pltpu.make_async_copy(b2, bias.at[1], local.at[9]))
    for load in loads[:2]:
        load.start()

    barrier = pltpu.get_barrier_semaphore()
    pl.semaphore_signal(barrier, inc=1, device_id=(sib, j), device_id_type=MESH)
    greeted = ((has_ext, (ext, j)), (has_up, (s, j - 1)), (has_down, (s, j + 1)))
    for there, who in greeted:
        @pl.when(there)
        def _(who=who):
            pl.semaphore_signal(barrier, inc=1, device_id=who, device_id_type=MESH)
    for load in loads[2:]:
        load.start()

    def clear(ref, place):
        ref[place] = jnp.zeros(ref.at[place].shape, BF16)

    for block, outer, above, below in ((one, slice(0, 2), (0, 1), (6, 7)), (two, 0, (0,), (5,))):
        pl.when(~has_ext)(lambda block=block, outer=outer: clear(block, (outer,)))
        for there, places in ((has_up, above), (has_down, below)):
            for place in places:
                pl.when(~there)(lambda block=block, place=place: clear(block, (slice(None), place)))

    used = []

    def remote(src, dst, to, sends, receives):
        n = len(used)
        copy = pltpu.make_async_remote_copy(
            src_ref=src, dst_ref=dst, send_sem=send_sems.at[n], recv_sem=recv_sems.at[n],
            device_id=to, device_id_type=MESH,
        )
        used.append((copy, sends, receives))
        return used[-1]

    def start(*copies):
        for copy, sends, _ in copies:
            copy.start() if sends is True else pl.when(sends)(copy.start)

    def arrived(*copies):
        for copy, _, receives in copies:
            copy.wait_recv() if receives is True else pl.when(receives)(copy.wait_recv)

    sibling, outside, above, below = (sib, j), (ext, j), (s, j - 1), (s, j + 1)
    to_sib = remote(one.at[3, OWN_ONE], one.at[4, OWN_ONE], sibling, True, True)
    to_ext = remote(one.at[2:4, OWN_ONE], one.at[0:2, OWN_ONE], outside, has_ext, has_ext)
    near = (
        remote(one.at[2:4, 2], one.at[2:4, 6], above, has_up, has_down),
        remote(one.at[2:4, 5], one.at[2:4, 1], below, has_down, has_up),
    )
    far = (
        remote(one.at[2:4, 3], one.at[2:4, 7], above, has_up, has_down),
        remote(one.at[2:4, 4], one.at[2:4, 0], below, has_down, has_up),
    )
    near_seam = (
        remote(one.at[0:2, 2], one.at[0:2, 6], above, seam & has_up, seam & has_down),
        remote(one.at[0:2, 5], one.at[0:2, 1], below, seam & has_down, seam & has_up),
    )
    far_seam = (
        remote(one.at[0:2, 3], one.at[0:2, 7], above, seam & has_up, seam & has_down),
        remote(one.at[0:2, 4], one.at[0:2, 0], below, seam & has_down, seam & has_up),
    )

    def corners(r_up, r_down):
        copies = []
        for r, there in ((r_up, has_up), (r_down, has_down)):
            passed = has_ext & ~seam & there
            copies.append(remote(one.at[2:4, r], one.at[0:2, r], outside, passed, passed))
            copies.append(remote(one.at[3, r], one.at[4, r], sibling, there, there))
        return copies

    near_corners, far_corners = corners(1, 6), corners(0, 7)
    inner_two = remote(two.at[2, OWN_TWO], two.at[3, OWN_TWO], sibling, True, True)
    outer_two = [remote(two.at[2, r], two.at[3, r], sibling, there, there) for r, there in ((0, has_up), (5, has_down))]
    own_slab = pl.ds(pl.multiple_of(j * SLAB, SLAB), SLAB)
    turns = []
    for n in range(2):
        turns.append([])
        for step in (2, 1, 3):
            to = (j + step) % CHAN
            turns[n].append(remote(
                mine.at[n, pl.ds(pl.multiple_of(to * SLAB, SLAB), SLAB)], got.at[n, j], (s, to), True, True
            ))

    loads[0].wait()
    loads[1].wait()
    pl.semaphore_wait(barrier, 1 + sum(there.astype(jnp.int32) for there, _ in greeted))
    pl.when(seam)(to_ext[0].start)
    start(*near)
    pl.when(has_ext & ~seam)(to_ext[0].start)
    start(to_sib, *far)

    arrived(*near)
    start(*near_corners)
    for at, tell in ((1, 0), (2, 3)):
        @pl.when(j == at)
        def _(tell=tell):
            pl.semaphore_signal(relay, inc=1, device_id=(s, tell), device_id_type=MESH)
    for load in loads[2:5] + loads[8:]:
        load.wait()
    bias1 = bias[0]

    def hidden(step, carry):
        @pl.when(step == 0)
        def _():
            arrived(to_ext)
            start(*near_seam, *far_seam)
            arrived(to_sib)

        @pl.when(step == 1)
        def _():
            arrived(*far)
            start(*far_corners)
            arrived(*near_corners, *near_seam)

        @pl.when(step == 2)
        def _():
            start(inner_two)
            arrived(*far_corners, *far_seam)

        sums = accumulate(one, PLANE_ONE, FIRST_ONE, (E1, O0, O1), step, w1, False)
        value = leaky(shifted_rows(*sums) + bias1).astype(BF16).reshape(3, 2, 64, 256)
        two[0:3, 2 - step] = value[:, 0]
        two[0:3, 3 + step] = value[:, 1]
        return carry

    lax.fori_loop(0, 3, hidden, 0)
    pl.when(~has_ext)(lambda: clear(two, (0,)))
    for there, r in ((has_up, 0), (has_down, 5)):
        pl.when(~there)(lambda r=r: clear(two, (slice(None), r)))
    start(*outer_two)
    for load in loads[5:8]:
        load.wait()
    bias2 = jnp.transpose(jnp.broadcast_to(bias[1], (8, 256)))[:, :1]
    arrived(inner_two)
    pl.when((j == 0) | (j == CHAN - 1))(lambda: pl.semaphore_wait(relay, 1))

    def features(step, carry):
        @pl.when(step == 1)
        def _():
            arrived(*outer_two)

        sums = accumulate(two, PLANE_TWO, FIRST_TWO, (O0, O1), step, w2, True)
        value = leaky(shifted_lanes(*sums) + bias2).astype(BF16)
        for q in range(2):
            p = q + flip * (1 - 2 * q)
            mine[step, :, pl.ds(pl.multiple_of(128 * p, 128), 128)] = value[:, 128 * q : 128 * q + 128]
        for n in range(2):
            pl.when(step == n)(lambda n=n: start(*turns[n]))
        pltpu.make_async_copy(mine.at[step, own_slab], got.at[step, j], local.at[10 + step]).start()
        return carry

    lax.fori_loop(0, 2, features, 0)
    for n in range(2):
        pltpu.make_async_copy(mine.at[n, own_slab], got.at[n, j], local.at[10 + n]).wait()
        arrived(*turns[n])
    for copy, sends, _ in used:
        copy.wait_send() if sends is True else pl.when(sends)(copy.wait_send)


def regroup(got, out):
    for p in range(2):
        rows = [None] * 16
        for n in range(2):
            for source in range(CHAN):
                pair = got[n, source, :, 128 * p : 128 * p + 128].astype(F32)
                rows[4 * source + 1 - n] = pair[:, :64]
                rows[4 * source + 2 + n] = pair[:, 64:]
        out[:, p] = pltpu.einshape("yoz->oyz", jnp.stack(rows, axis=0)).astype(BF16)


def on_device(volume, first_filter, first_bias, second_filter, second_bias):
    voxels = jnp.transpose(volume, (1, 2, 3, 0))
    hbm = pl.BlockSpec(memory_space=pltpu.HBM)
    dma = pltpu.SemaphoreType.DMA
    got = pl.pallas_call(
        kernel,
        out_shape=jax.ShapeDtypeStruct((2, CHAN, SLAB, 256), BF16),
        in_specs=[hbm] * 5,
        out_specs=hbm,
        scratch_shapes=[
            pltpu.VMEM((5, 8, 64, 256), BF16),
            pltpu.VMEM((4, 6, 64, 256), BF16),
            pltpu.VMEM((27, 256, 256), BF16),
            pltpu.VMEM((27, 256, 256), BF16),
            pltpu.VMEM((2, 1, 256), F32),
            pltpu.VMEM((2, 256, 256), BF16),
            dma((12,)),
            dma((27,)),
            dma((27,)),
            pltpu.SemaphoreType.REGULAR,
        ],
        compiler_params=pltpu.CompilerParams(
            collective_id=0, has_side_effects=True, vmem_limit_bytes=62 * 2**20
        ),
        cost_estimate=pl.CostEstimate(flops=5_900_000_000, bytes_accessed=8_000_000, transcendentals=0),
    )(voxels, first_filter, first_bias.reshape(1, 256), second_filter, second_bias.reshape(1, 256))
    part = SLAB // 2
    return pl.pallas_call(
        regroup,
        out_shape=jax.ShapeDtypeStruct((SLAB, 2, 16, 64), BF16),
        grid=(2,),
        in_specs=[pl.BlockSpec((2, CHAN, part, 256), lambda i: (0, 0, i, 0))],
        out_specs=pl.BlockSpec((part, 2, 16, 64), lambda i: (i, 0, 0, 0)),
        cost_estimate=pl.CostEstimate(flops=0, bytes_accessed=786432, transcendentals=0),
    )(got)


def solution(mesh):
    in_specs = (P(None, "space", "chan", None), P(), P(), P(), P())
    out_specs = P("chan", "space", None, None)
    return jax.shard_map(
        on_device, mesh=mesh, in_specs=in_specs, out_specs=out_specs, check_vma=False
    )
```

```python
import jax
import jax.numpy as jnp
from jax import lax
from jax.experimental import pallas as pl
from jax.experimental.pallas import tpu as pltpu
from jax.sharding import PartitionSpec as P

MESH = pl.DeviceIdType.MESH
F32, BF16 = jnp.float32, jnp.bfloat16
CHAN = 4
SLAB = 64
E2, E1, O0, O1, I1 = range(-2, 3)
PLANE_ONE = {E1: 0, E2: 1, O0: 2, O1: 3, I1: 4}
PLANE_TWO = {E1: 0, O0: 1, O1: 2, I1: 3}
OWN_ONE, OWN_TWO = slice(2, 6), slice(1, 5)


def leaky(value):
    return jnp.where(value >= 0.0, value, 0.3 * value)


def nt(a, b):
    return lax.dot_general(a, b, (((1,), (1,)), ((), ())), preferred_element_type=F32)


def shifted_rows(low, mid, high):
    rows = low.shape[0]
    z = lax.broadcasted_iota(jnp.int32, low.shape, 0) % 64
    up = jnp.where(z == 0, 0.0, pltpu.roll(low, 1, 0))
    down = jnp.where(z == 63, 0.0, pltpu.roll(high, rows - 1, 0))
    return mid + up + down


def shifted_lanes(low, mid, high):
    parts = []
    for first in range(0, low.shape[1], 128):
        cut = slice(first, first + 128)
        z = lax.broadcasted_iota(jnp.int32, (low.shape[0], 128), 1) % 64
        up = jnp.where(z == 0, 0.0, pltpu.roll(low[:, cut], 1, 1))
        down = jnp.where(z == 63, 0.0, pltpu.roll(high[:, cut], 127, 1))
        parts.append(mid[:, cut] + up + down)
    return jnp.concatenate(parts, axis=1)


def accumulate(block, pieces, filters, channels_first):
    sums = [None] * 3
    for a in range(3):
        for b in range(3):
            voxels = jnp.concatenate([block[place] for place in pieces(a, b)], axis=0)
            for c in range(3):
                taps = filters[9 * a + 3 * b + c]
                term = nt(taps, voxels) if channels_first else nt(voxels, taps)
                sums[c] = term if sums[c] is None else sums[c] + term
    return sums


def kernel(
    vol, f1, b1, f2, b2, got,
    one, two, w1, w2, bias, mine, local, send_sems, recv_sems, relay,
):
    s, j = lax.axis_index("space"), lax.axis_index("chan")
    flip = s % 2
    sib, ext = s + 1 - 2 * flip, s - 1 + 2 * flip
    has_ext = (ext >= 0) & (ext < lax.axis_size("space"))
    has_up, has_down = j > 0, j < CHAN - 1
    half = lax.axis_size("space") // 2
    seam = (s == half - 1) | (s == half)

    loads = [
        pltpu.make_async_copy(vol.at[flip], one.at[2, OWN_ONE], local.at[0]),
        pltpu.make_async_copy(vol.at[1 - flip], one.at[3, OWN_ONE], local.at[1]),
    ]
    for n, (src, dst) in enumerate(((f1, w1), (f2, w2))):
        for a in range(3):
            first = 9 * (a + flip * (2 - 2 * a))
            loads.append(pltpu.make_async_copy(src.at[pl.ds(first, 9)], dst.at[9 * a : 9 * a + 9], local.at[2 + 3 * n + a]))
    loads.append(pltpu.make_async_copy(b1, bias.at[0], local.at[8]))
    loads.append(pltpu.make_async_copy(b2, bias.at[1], local.at[9]))
    for load in loads[:2]:
        load.start()

    barrier = pltpu.get_barrier_semaphore()
    pl.semaphore_signal(barrier, inc=1, device_id=(sib, j), device_id_type=MESH)
    greeted = ((has_ext, (ext, j)), (has_up, (s, j - 1)), (has_down, (s, j + 1)))
    for there, who in greeted:
        @pl.when(there)
        def _(who=who):
            pl.semaphore_signal(barrier, inc=1, device_id=who, device_id_type=MESH)
    for load in loads[2:]:
        load.start()

    def clear(ref, place):
        ref[place] = jnp.zeros(ref.at[place].shape, BF16)

    pl.when(~has_ext)(lambda: clear(one, (slice(0, 2),)))
    for there, places in ((has_up, (0, 1)), (has_down, (6, 7))):
        for place in places:
            pl.when(~there)(lambda place=place: clear(one, (slice(None), place)))

    used = []

    def remote(src, dst, to, sends, receives):
        n = len(used)
        copy = pltpu.make_async_remote_copy(
            src_ref=src, dst_ref=dst, send_sem=send_sems.at[n], recv_sem=recv_sems.at[n],
            device_id=to, device_id_type=MESH,
        )
        used.append((copy, sends, receives))
        return used[-1]

    def start(*copies):
        for copy, sends, _ in copies:
            copy.start() if sends is True else pl.when(sends)(copy.start)

    def arrived(*copies):
        for copy, _, receives in copies:
            copy.wait_recv() if receives is True else pl.when(receives)(copy.wait_recv)

    sibling, outside, above, below = (sib, j), (ext, j), (s, j - 1), (s, j + 1)
    to_sib = remote(one.at[3, OWN_ONE], one.at[4, OWN_ONE], sibling, True, True)
    to_ext = remote(one.at[2:4, OWN_ONE], one.at[0:2, OWN_ONE], outside, has_ext, has_ext)
    near = (
        remote(one.at[2:4, 2], one.at[2:4, 6], above, has_up, has_down),
        remote(one.at[2:4, 5], one.at[2:4, 1], below, has_down, has_up),
    )
    far = (
        remote(one.at[2:4, 3], one.at[2:4, 7], above, has_up, has_down),
        remote(one.at[2:4, 4], one.at[2:4, 0], below, has_down, has_up),
    )
    near_seam = (
        remote(one.at[0:2, 2], one.at[0:2, 6], above, seam & has_up, seam & has_down),
        remote(one.at[0:2, 5], one.at[0:2, 1], below, seam & has_down, seam & has_up),
    )
    far_seam = (
        remote(one.at[0:2, 3], one.at[0:2, 7], above, seam & has_up, seam & has_down),
        remote(one.at[0:2, 4], one.at[0:2, 0], below, seam & has_down, seam & has_up),
    )

    def corners(r_up, r_down):
        outward, inward = [], []
        for r, there in ((r_up, has_up), (r_down, has_down)):
            passed = has_ext & ~seam & there
            outward.append(remote(one.at[2:4, r], one.at[0:2, r], outside, passed, passed))
            inward.append(remote(one.at[3, r], one.at[4, r], sibling, there, there))
        return outward, inward

    near_outward, near_inward = corners(1, 6)
    far_outward, far_inward = corners(0, 7)
    plane_two = remote(two.at[2], two.at[3], sibling, True, True)
    own_slab = pl.ds(pl.multiple_of(j * SLAB, SLAB), SLAB)
    turns = []
    for n in range(2):
        turns.append([])
        for step in (2, 1, 3):
            to = (j + step) % CHAN
            turns[n].append(remote(
                mine.at[n, pl.ds(pl.multiple_of(to * SLAB, SLAB), SLAB)], got.at[n, j], (s, to), True, True
            ))

    loads[0].wait()
    loads[1].wait()
    pl.semaphore_wait(barrier, 1 + sum(there.astype(jnp.int32) for there, _ in greeted))
    pl.when(seam)(to_ext[0].start)
    start(*near)
    pl.when(has_ext & ~seam)(to_ext[0].start)
    busy = ((s + 2) % half < 4) & ~seam
    start(to_sib)
    for copy, sends, _ in far:
        pl.when(sends & ~busy)(copy.start)

    arrived(*near)
    start(*near_outward, *near_inward)
    for copy, sends, _ in far:
        pl.when(sends & busy)(copy.start)
    for at, tell in ((1, 0), (2, 3)):
        @pl.when(j == at)
        def _(tell=tell):
            pl.semaphore_signal(relay, inc=1, device_id=(s, tell), device_id_type=MESH)
    for load in loads[2:5] + loads[8:]:
        load.wait()
    bias1 = bias[0]
    arrived(to_ext)
    start(*near_seam, *far_seam)
    arrived(to_sib)

    def hidden(pieces):
        return leaky(shifted_rows(*accumulate(one, pieces, w1, False)) + bias1).astype(BF16).reshape(-1, 64, 256)

    value = hidden(lambda a, b: [(PLANE_ONE[p + a - 1], y + b + 1) for p in (E1, O0, O1) for y in (1, 2)])
    two[0:3, 2:4] = value.reshape(3, 2, 64, 256)
    for load in loads[5:8]:
        load.wait()
    bias2 = jnp.transpose(jnp.broadcast_to(bias[1], (8, 256)))[:, :1]

    def clear_rows(planes):
        for there, r in ((has_up, 0), (has_down, 5)):
            pl.when(~there)(lambda r=r: clear(two, (planes, r)))

    def block(step, carry):
        @pl.when(step == 0)
        def _():
            arrived(*far)
            start(*far_outward, *far_inward)
            arrived(*near_inward, *far_inward)

        @pl.when(step == 1)
        def _():
            arrived(*near_outward, *near_seam)

        @pl.when(step == 2)
        def _():
            arrived(*far_outward, *far_seam)

        at_o1 = (2 - step) // 2
        rows = (-(step // 2), 3 + step // 2, step % 2 - 1, 4 - step % 2)

        def place(a, i):
            other = PLANE_ONE[(O0, E1)[i // 2] + a - 1]
            return other + at_o1 * (PLANE_ONE[O1 + a - 1] - other)

        value = hidden(lambda a, b: [(place(a, i), rows[i] + b + 1) for i in range(4)])
        for i in range(4):
            other = PLANE_TWO[(O0, E1)[i // 2]]
            two[other + at_o1 * (PLANE_TWO[O1] - other), rows[i] + 1] = value[i]

        @pl.when(step == 0)
        def _():
            clear_rows(2)
            start(plane_two)

        @pl.when(step == 1)
        def _():
            pl.when(~has_ext)(lambda: clear(two, (0,)))
            arrived(plane_two)
            pl.when((j == 0) | (j == CHAN - 1))(lambda: pl.semaphore_wait(relay, 1))

        @pl.when(step == 2)
        def _():
            pl.when(~has_ext)(lambda: clear(two, (0,)))
            clear_rows(slice(0, 2))

        pl.when(step > 0)(lambda: features(step - 1))
        return carry

    def features(n):
        pieces = lambda a, b: [(PLANE_TWO[p + a - 1], y + b) for p in (O0, O1) for y in (1 - n, 2 + n)]
        value = leaky(shifted_lanes(*accumulate(two, pieces, w2, True)) + bias2).astype(BF16)
        for q in range(2):
            p = q + flip * (1 - 2 * q)
            mine[n, :, pl.ds(pl.multiple_of(128 * p, 128), 128)] = value[:, 128 * q : 128 * q + 128]
        for k in range(2):
            pl.when(n == k)(lambda k=k: start(*turns[k]))
        pltpu.make_async_copy(mine.at[n, own_slab], got.at[n, j], local.at[10 + n]).start()

    lax.fori_loop(0, 3, block, 0)
    for n in range(2):
        pltpu.make_async_copy(mine.at[n, own_slab], got.at[n, j], local.at[10 + n]).wait()
        arrived(*turns[n])
    for copy, sends, _ in used:
        copy.wait_send() if sends is True else pl.when(sends)(copy.wait_send)


def regroup(got, out):
    for p in range(2):
        rows = [None] * 16
        for n in range(2):
            for source in range(CHAN):
                pair = got[n, source, :, 128 * p : 128 * p + 128].astype(F32)
                rows[4 * source + 1 - n] = pair[:, :64]
                rows[4 * source + 2 + n] = pair[:, 64:]
        out[:, p] = pltpu.einshape("yoz->oyz", jnp.stack(rows, axis=0)).astype(BF16)


def on_device(volume, first_filter, first_bias, second_filter, second_bias):
    voxels = jnp.transpose(volume, (1, 2, 3, 0))
    hbm = pl.BlockSpec(memory_space=pltpu.HBM)
    dma = pltpu.SemaphoreType.DMA
    got = pl.pallas_call(
        kernel,
        out_shape=jax.ShapeDtypeStruct((2, CHAN, SLAB, 256), BF16),
        in_specs=[hbm] * 5,
        out_specs=hbm,
        scratch_shapes=[
            pltpu.VMEM((5, 8, 64, 256), BF16),
            pltpu.VMEM((4, 6, 64, 256), BF16),
            pltpu.VMEM((27, 256, 256), BF16),
            pltpu.VMEM((27, 256, 256), BF16),
            pltpu.VMEM((2, 1, 256), F32),
            pltpu.VMEM((2, 256, 256), BF16),
            dma((12,)),
            dma((28,)),
            dma((28,)),
            pltpu.SemaphoreType.REGULAR,
        ],
        compiler_params=pltpu.CompilerParams(
            collective_id=0, has_side_effects=True, vmem_limit_bytes=62 * 2**20
        ),
        cost_estimate=pl.CostEstimate(flops=5_900_000_000, bytes_accessed=8_000_000, transcendentals=0),
    )(voxels, first_filter, first_bias.reshape(1, 256), second_filter, second_bias.reshape(1, 256))
    part = SLAB // 2
    return pl.pallas_call(
        regroup,
        out_shape=jax.ShapeDtypeStruct((SLAB, 2, 16, 64), BF16),
        grid=(2,),
        in_specs=[pl.BlockSpec((2, CHAN, part, 256), lambda i: (0, 0, i, 0))],
        out_specs=pl.BlockSpec((part, 2, 16, 64), lambda i: (i, 0, 0, 0)),
        cost_estimate=pl.CostEstimate(flops=0, bytes_accessed=786432, transcendentals=0),
    )(got)


def solution(mesh):
    in_specs = (P(None, "space", "chan", None), P(), P(), P(), P())
    out_specs = P("chan", "space", None, None)
    return jax.shard_map(
        on_device, mesh=mesh, in_specs=in_specs, out_specs=out_specs, check_vma=False
    )
```

```python
import jax
import jax.numpy as jnp
from jax import lax
from jax.experimental import pallas as pl
from jax.experimental.pallas import tpu as pltpu
from jax.sharding import PartitionSpec as P

MESH = pl.DeviceIdType.MESH
F32, BF16 = jnp.float32, jnp.bfloat16
CHAN = 4
SLAB = 64
E2, E1, O0, O1, I1 = range(-2, 3)
PLANE_ONE = {E1: 0, E2: 1, O0: 2, O1: 3, I1: 4}
PLANE_TWO = {E1: 0, O0: 1, O1: 2, I1: 3}
OWN_ONE = slice(2, 6)


def leaky(value):
    return jnp.where(value >= 0.0, value, 0.3 * value)


def nt(a, b):
    return lax.dot_general(a, b, (((1,), (1,)), ((), ())), preferred_element_type=F32)


def shifted_rows(low, mid, high):
    rows = low.shape[0]
    z = lax.broadcasted_iota(jnp.int32, low.shape, 0) % 64
    up = jnp.where(z == 0, 0.0, pltpu.roll(low, 1, 0))
    down = jnp.where(z == 63, 0.0, pltpu.roll(high, rows - 1, 0))
    return mid + up + down


def shifted_lanes(low, mid, high):
    parts = []
    for first in range(0, low.shape[1], 128):
        cut = slice(first, first + 128)
        z = lax.broadcasted_iota(jnp.int32, (low.shape[0], 128), 1) % 64
        up = jnp.where(z == 0, 0.0, pltpu.roll(low[:, cut], 1, 1))
        down = jnp.where(z == 63, 0.0, pltpu.roll(high[:, cut], 127, 1))
        parts.append(mid[:, cut] + up + down)
    return jnp.concatenate(parts, axis=1)


def accumulate(block, pieces, filters, channels_first):
    sums = [None] * 3
    for a in range(3):
        for b in range(3):
            voxels = jnp.concatenate([block[place] for place in pieces(a, b)], axis=0)
            for c in range(3):
                taps = filters[9 * a + 3 * b + c]
                term = nt(taps, voxels) if channels_first else nt(voxels, taps)
                sums[c] = term if sums[c] is None else sums[c] + term
    return sums


def kernel(
    vol, f1, b1, f2, b2, got,
    one, two, w1, w2, bias, mine, local, send_sems, recv_sems, relay,
):
    s, j = lax.axis_index("space"), lax.axis_index("chan")
    flip = s % 2
    sib, ext = s + 1 - 2 * flip, s - 1 + 2 * flip
    has_ext = (ext >= 0) & (ext < lax.axis_size("space"))
    has_up, has_down = j > 0, j < CHAN - 1
    half = lax.axis_size("space") // 2
    seam = (s == half - 1) | (s == half)

    loads = [
        pltpu.make_async_copy(vol.at[flip], one.at[2, OWN_ONE], local.at[0]),
        pltpu.make_async_copy(vol.at[1 - flip], one.at[3, OWN_ONE], local.at[1]),
    ]
    for n, (src, dst) in enumerate(((f1, w1), (f2, w2))):
        for a in range(3):
            first = 9 * (a + flip * (2 - 2 * a))
            loads.append(pltpu.make_async_copy(src.at[pl.ds(first, 9)], dst.at[9 * a : 9 * a + 9], local.at[2 + 3 * n + a]))
    loads.append(pltpu.make_async_copy(b1, bias.at[0], local.at[8]))
    loads.append(pltpu.make_async_copy(b2, bias.at[1], local.at[9]))
    for load in loads[:2]:
        load.start()

    barrier = pltpu.get_barrier_semaphore()
    pl.semaphore_signal(barrier, inc=1, device_id=(sib, j), device_id_type=MESH)
    greeted = ((has_ext, (ext, j)), (has_up, (s, j - 1)), (has_down, (s, j + 1)))
    for there, who in greeted:
        @pl.when(there)
        def _(who=who):
            pl.semaphore_signal(barrier, inc=1, device_id=who, device_id_type=MESH)
    for load in loads[2:]:
        load.start()

    def clear(ref, place):
        ref[place] = jnp.zeros(ref.at[place].shape, BF16)

    pl.when(~has_ext)(lambda: clear(one, (slice(0, 2),)))
    for there, places in ((has_up, (0, 1)), (has_down, (6, 7))):
        for place in places:
            pl.when(~there)(lambda place=place: clear(one, (slice(None), place)))

    used = []

    def remote(src, dst, to, sends, receives):
        n = len(used)
        copy = pltpu.make_async_remote_copy(
            src_ref=src, dst_ref=dst, send_sem=send_sems.at[n], recv_sem=recv_sems.at[n],
            device_id=to, device_id_type=MESH,
        )
        used.append((copy, sends, receives))
        return used[-1]

    def start(*copies):
        for copy, sends, _ in copies:
            copy.start() if sends is True else pl.when(sends)(copy.start)

    def arrived(*copies):
        for copy, _, receives in copies:
            copy.wait_recv() if receives is True else pl.when(receives)(copy.wait_recv)

    sibling, outside, above, below = (sib, j), (ext, j), (s, j - 1), (s, j + 1)
    to_sib = remote(one.at[3, OWN_ONE], one.at[4, OWN_ONE], sibling, True, True)
    to_ext = remote(one.at[2:4, OWN_ONE], one.at[0:2, OWN_ONE], outside, has_ext, has_ext)
    near = (
        remote(one.at[2:4, 2], one.at[2:4, 6], above, has_up, has_down),
        remote(one.at[2:4, 5], one.at[2:4, 1], below, has_down, has_up),
    )
    far = (
        remote(one.at[2:4, 3], one.at[2:4, 7], above, has_up, has_down),
        remote(one.at[2:4, 4], one.at[2:4, 0], below, has_down, has_up),
    )
    far_seam = (
        remote(one.at[0:2, 3], one.at[0:2, 7], above, seam & has_up, seam & has_down),
        remote(one.at[0:2, 4], one.at[0:2, 0], below, seam & has_down, seam & has_up),
    )

    def corners(r_up, r_down, outer):
        outward, inward = [], []
        for r, there in ((r_up, has_up), (r_down, has_down)):
            passed = outer & there
            outward.append(remote(one.at[2:4, r], one.at[0:2, r], outside, passed, passed))
            inward.append(remote(one.at[3, r], one.at[4, r], sibling, there, there))
        return outward, inward

    near_outward, near_inward = corners(1, 6, has_ext)
    far_outward, far_inward = corners(0, 7, has_ext & ~seam)
    plane_two = remote(two.at[2], two.at[3], sibling, True, True)
    own_slab = pl.ds(pl.multiple_of(j * SLAB, SLAB), SLAB)
    turns = []
    for n in range(2):
        turns.append([])
        for step in (2, 1, 3):
            to = (j + step) % CHAN
            turns[n].append(remote(
                mine.at[n, pl.ds(pl.multiple_of(to * SLAB, SLAB), SLAB)], got.at[n, j], (s, to), True, True
            ))

    loads[0].wait()
    loads[1].wait()
    pl.semaphore_wait(barrier, 1 + sum(there.astype(jnp.int32) for there, _ in greeted))
    pl.when(seam)(to_ext[0].start)
    start(*near)
    pl.when(has_ext & ~seam)(to_ext[0].start)
    busy = ((s + 2) % half < 4) & ~seam
    start(to_sib)
    for copy, sends, _ in far:
        pl.when(sends & ~busy)(copy.start)

    arrived(*near)
    start(*near_outward, *near_inward)
    for copy, sends, _ in far:
        pl.when(sends & busy)(copy.start)
    for at, tell in ((1, 0), (2, 3)):
        @pl.when(j == at)
        def _(tell=tell):
            pl.semaphore_signal(relay, inc=1, device_id=(s, tell), device_id_type=MESH)
    for load in loads[2:5] + loads[8:]:
        load.wait()
    bias1 = bias[0]
    arrived(to_ext)
    start(*far_seam)
    arrived(to_sib)

    def hidden(pieces):
        return leaky(shifted_rows(*accumulate(one, pieces, w1, False)) + bias1).astype(BF16).reshape(-1, 64, 256)

    value = hidden(lambda a, b: [(PLANE_ONE[p + a - 1], y + b + 1) for p in (E1, O0, O1) for y in (1, 2)])
    two[0:3, 2:4] = value.reshape(3, 2, 64, 256)
    for load in loads[5:8]:
        load.wait()
    bias2 = jnp.transpose(jnp.broadcast_to(bias[1], (8, 256)))[:, :1]

    def clear_rows(planes):
        for there, r in ((has_up, 0), (has_down, 5)):
            pl.when(~there)(lambda r=r: clear(two, (planes, r)))

    def block(step, carry):
        @pl.when(step == 0)
        def _():
            arrived(*far)
            start(*far_outward, *far_inward)
            arrived(*near_inward, *far_inward)

        @pl.when(step == 1)
        def _():
            arrived(*near_outward)

        @pl.when(step == 2)
        def _():
            arrived(*far_outward, *far_seam)

        at_o1 = (2 - step) // 2
        rows = (-(step // 2), 3 + step // 2, step % 2 - 1, 4 - step % 2)

        def place(a, i):
            other = PLANE_ONE[(O0, E1)[i // 2] + a - 1]
            return other + at_o1 * (PLANE_ONE[O1 + a - 1] - other)

        value = hidden(lambda a, b: [(place(a, i), rows[i] + b + 1) for i in range(4)])
        for i in range(4):
            other = PLANE_TWO[(O0, E1)[i // 2]]
            two[other + at_o1 * (PLANE_TWO[O1] - other), rows[i] + 1] = value[i]

        @pl.when(step == 0)
        def _():
            clear_rows(2)
            start(plane_two)

        @pl.when(step == 1)
        def _():
            pl.when(~has_ext)(lambda: clear(two, (0,)))
            arrived(plane_two)
            pl.when((j == 0) | (j == CHAN - 1))(lambda: pl.semaphore_wait(relay, 1))

        @pl.when(step == 2)
        def _():
            pl.when(~has_ext)(lambda: clear(two, (0,)))
            clear_rows(slice(0, 2))

        pl.when(step > 0)(lambda: features(step - 1))
        return carry

    def features(n):
        pieces = lambda a, b: [(PLANE_TWO[p + a - 1], y + b) for p in (O0, O1) for y in (1 - n, 2 + n)]
        value = leaky(shifted_lanes(*accumulate(two, pieces, w2, True)) + bias2).astype(BF16)
        for q in range(2):
            p = q + flip * (1 - 2 * q)
            mine[n, :, pl.ds(pl.multiple_of(128 * p, 128), 128)] = value[:, 128 * q : 128 * q + 128]
        for k in range(2):
            pl.when(n == k)(lambda k=k: start(*turns[k]))
        pltpu.make_async_copy(mine.at[n, own_slab], got.at[n, j], local.at[10 + n]).start()

    lax.fori_loop(0, 3, block, 0)
    for n in range(2):
        pltpu.make_async_copy(mine.at[n, own_slab], got.at[n, j], local.at[10 + n]).wait()
        arrived(*turns[n])
    for copy, sends, _ in used:
        copy.wait_send() if sends is True else pl.when(sends)(copy.wait_send)


def regroup(got, out):
    for p in range(2):
        rows = [None] * 16
        for n in range(2):
            for source in range(CHAN):
                pair = got[n, source, :, 128 * p : 128 * p + 128].astype(F32)
                rows[4 * source + 1 - n] = pair[:, :64]
                rows[4 * source + 2 + n] = pair[:, 64:]
        out[:, p] = pltpu.einshape("yoz->oyz", jnp.stack(rows, axis=0)).astype(BF16)


def on_device(volume, first_filter, first_bias, second_filter, second_bias):
    voxels = jnp.transpose(volume, (1, 2, 3, 0))
    hbm = pl.BlockSpec(memory_space=pltpu.HBM)
    dma = pltpu.SemaphoreType.DMA
    got = pl.pallas_call(
        kernel,
        out_shape=jax.ShapeDtypeStruct((2, CHAN, SLAB, 256), BF16),
        in_specs=[hbm] * 5,
        out_specs=hbm,
        scratch_shapes=[
            pltpu.VMEM((5, 8, 64, 256), BF16),
            pltpu.VMEM((4, 6, 64, 256), BF16),
            pltpu.VMEM((27, 256, 256), BF16),
            pltpu.VMEM((27, 256, 256), BF16),
            pltpu.VMEM((2, 1, 256), F32),
            pltpu.VMEM((2, 256, 256), BF16),
            dma((12,)),
            dma((26,)),
            dma((26,)),
            pltpu.SemaphoreType.REGULAR,
        ],
        compiler_params=pltpu.CompilerParams(
            collective_id=0, has_side_effects=True, vmem_limit_bytes=62 * 2**20
        ),
        cost_estimate=pl.CostEstimate(flops=5_900_000_000, bytes_accessed=8_000_000, transcendentals=0),
    )(voxels, first_filter, first_bias.reshape(1, 256), second_filter, second_bias.reshape(1, 256))
    part = SLAB // 2
    return pl.pallas_call(
        regroup,
        out_shape=jax.ShapeDtypeStruct((SLAB, 2, 16, 64), BF16),
        grid=(2,),
        in_specs=[pl.BlockSpec((2, CHAN, part, 256), lambda i: (0, 0, i, 0))],
        out_specs=pl.BlockSpec((part, 2, 16, 64), lambda i: (i, 0, 0, 0)),
        cost_estimate=pl.CostEstimate(flops=0, bytes_accessed=786432, transcendentals=0),
    )(got)


def solution(mesh):
    in_specs = (P(None, "space", "chan", None), P(), P(), P(), P())
    out_specs = P("chan", "space", None, None)
    return jax.shard_map(
        on_device, mesh=mesh, in_specs=in_specs, out_specs=out_specs, check_vma=False
    )
```

```python
import jax
import jax.numpy as jnp
from jax import lax
from jax.experimental import pallas as pl
from jax.experimental.pallas import tpu as pltpu
from jax.sharding import PartitionSpec as P

MESH = pl.DeviceIdType.MESH
F32, BF16 = jnp.float32, jnp.bfloat16
CHAN = 4
SLAB = 64
E2, E1, O0, O1, I1 = range(-2, 3)
PLANE_ONE = {E1: 0, E2: 1, O0: 2, O1: 3, I1: 4}
PLANE_TWO = {E1: 0, O0: 1, O1: 2, I1: 3}
OWN_ONE = slice(2, 6)


def leaky(value):
    return jnp.where(value >= 0.0, value, 0.3 * value)


def nt(a, b):
    return lax.dot_general(a, b, (((1,), (1,)), ((), ())), preferred_element_type=F32)


def shifted_rows(low, mid, high):
    rows = low.shape[0]
    z = lax.broadcasted_iota(jnp.int32, low.shape, 0) % 64
    up = jnp.where(z == 0, 0.0, pltpu.roll(low, 1, 0))
    down = jnp.where(z == 63, 0.0, pltpu.roll(high, rows - 1, 0))
    return mid + up + down


def shifted_lanes(low, mid, high):
    parts = []
    for first in range(0, low.shape[1], 128):
        cut = slice(first, first + 128)
        z = lax.broadcasted_iota(jnp.int32, (low.shape[0], 128), 1) % 64
        up = jnp.where(z == 0, 0.0, pltpu.roll(low[:, cut], 1, 1))
        down = jnp.where(z == 63, 0.0, pltpu.roll(high[:, cut], 127, 1))
        parts.append(mid[:, cut] + up + down)
    return jnp.concatenate(parts, axis=1)


def accumulate(block, pieces, filters, channels_first):
    sums = [None] * 3
    for a in range(3):
        for b in range(3):
            voxels = jnp.concatenate([block[place] for place in pieces(a, b)], axis=0)
            for c in range(3):
                taps = filters[9 * a + 3 * b + c]
                term = nt(taps, voxels) if channels_first else nt(voxels, taps)
                sums[c] = term if sums[c] is None else sums[c] + term
    return sums


def kernel(
    vol, f1, b1, f2, b2, got,
    one, two, w1, w2, bias, mine, local, send_sems, recv_sems, relay,
):
    s, j = lax.axis_index("space"), lax.axis_index("chan")
    flip = s % 2
    sib, ext = s + 1 - 2 * flip, s - 1 + 2 * flip
    has_ext = (ext >= 0) & (ext < lax.axis_size("space"))
    has_up, has_down = j > 0, j < CHAN - 1
    half = lax.axis_size("space") // 2
    seam = (s == half - 1) | (s == half)

    loads = [
        pltpu.make_async_copy(vol.at[flip], one.at[2, OWN_ONE], local.at[0]),
        pltpu.make_async_copy(vol.at[1 - flip], one.at[3, OWN_ONE], local.at[1]),
    ]
    for n, (src, dst) in enumerate(((f1, w1), (f2, w2))):
        for a in range(3):
            first = 9 * (a + flip * (2 - 2 * a))
            loads.append(pltpu.make_async_copy(src.at[pl.ds(first, 9)], dst.at[9 * a : 9 * a + 9], local.at[2 + 3 * n + a]))
    loads.append(pltpu.make_async_copy(b1, bias.at[0], local.at[8]))
    loads.append(pltpu.make_async_copy(b2, bias.at[1], local.at[9]))
    for load in loads[:2]:
        load.start()

    barrier = pltpu.get_barrier_semaphore()
    pl.semaphore_signal(barrier, inc=1, device_id=(sib, j), device_id_type=MESH)
    greeted = ((has_ext, (ext, j)), (has_up, (s, j - 1)), (has_down, (s, j + 1)))
    for there, who in greeted:
        @pl.when(there)
        def _(who=who):
            pl.semaphore_signal(barrier, inc=1, device_id=who, device_id_type=MESH)
    for load in loads[2:]:
        load.start()

    def clear(ref, place):
        ref[place] = jnp.zeros(ref.at[place].shape, BF16)

    pl.when(~has_ext)(lambda: clear(one, (slice(0, 2),)))
    for there, places in ((has_up, (0, 1)), (has_down, (6, 7))):
        for place in places:
            pl.when(~there)(lambda place=place: clear(one, (slice(None), place)))

    used = []

    def remote(src, dst, to, sends, receives):
        n = len(used)
        copy = pltpu.make_async_remote_copy(
            src_ref=src, dst_ref=dst, send_sem=send_sems.at[n], recv_sem=recv_sems.at[n],
            device_id=to, device_id_type=MESH,
        )
        used.append((copy, sends, receives))
        return used[-1]

    def start(*copies):
        for copy, sends, _ in copies:
            copy.start() if sends is True else pl.when(sends)(copy.start)

    def arrived(*copies):
        for copy, _, receives in copies:
            copy.wait_recv() if receives is True else pl.when(receives)(copy.wait_recv)

    sibling, outside, above, below = (sib, j), (ext, j), (s, j - 1), (s, j + 1)
    to_sib = remote(one.at[3, OWN_ONE], one.at[4, OWN_ONE], sibling, True, True)
    to_ext = remote(one.at[2:4, OWN_ONE], one.at[0:2, OWN_ONE], outside, has_ext, has_ext)
    near = (
        remote(one.at[2:4, 2], one.at[2:4, 6], above, has_up, has_down),
        remote(one.at[2:4, 5], one.at[2:4, 1], below, has_down, has_up),
    )
    far = (
        remote(one.at[2:4, 3], one.at[2:4, 7], above, has_up, has_down),
        remote(one.at[2:4, 4], one.at[2:4, 0], below, has_down, has_up),
    )
    far_seam = (
        remote(one.at[0:2, 3], one.at[0:2, 7], above, seam & has_up, seam & has_down),
        remote(one.at[0:2, 4], one.at[0:2, 0], below, seam & has_down, seam & has_up),
    )

    def corners(r_up, r_down, outer):
        outward, inward = [], []
        for r, there in ((r_up, has_up), (r_down, has_down)):
            passed = outer & there
            outward.append(remote(one.at[2:4, r], one.at[0:2, r], outside, passed, passed))
            inward.append(remote(one.at[3, r], one.at[4, r], sibling, there, there))
        return outward, inward

    near_outward, near_inward = corners(1, 6, has_ext)
    far_outward, far_inward = corners(0, 7, has_ext & ~seam)
    plane_two = remote(two.at[2], two.at[3], sibling, True, True)
    own_slab = pl.ds(pl.multiple_of(j * SLAB, SLAB), SLAB)
    turns = []
    for n in range(2):
        turns.append([])
        for step in (2, 1, 3):
            to = (j + step) % CHAN
            turns[n].append(remote(
                mine.at[n, pl.ds(pl.multiple_of(to * SLAB, SLAB), SLAB)], got.at[n, j], (s, to), True, True
            ))

    loads[0].wait()
    loads[1].wait()
    pl.semaphore_wait(barrier, 1 + sum(there.astype(jnp.int32) for there, _ in greeted))
    pl.when(seam)(to_ext[0].start)
    start(*near)
    pl.when(has_ext & ~seam)(to_ext[0].start)
    busy = ((s + 2) % half < 4) & ~seam
    start(to_sib)
    for copy, sends, _ in far:
        pl.when(sends & ~busy)(copy.start)

    arrived(*near)
    start(*near_outward, *near_inward)
    for copy, sends, _ in far:
        pl.when(sends & busy)(copy.start)
    for at, tell in ((1, 0), (2, 3)):
        @pl.when(j == at)
        def _(tell=tell):
            pl.semaphore_signal(relay, inc=1, device_id=(s, tell), device_id_type=MESH)
    for load in loads[2:5] + loads[8:]:
        load.wait()
    bias1 = bias[0]
    arrived(to_ext)
    start(*far_seam)
    arrived(to_sib)

    def hidden(pieces):
        return leaky(shifted_rows(*accumulate(one, pieces, w1, False)) + bias1).astype(BF16).reshape(-1, 64, 256)

    value = hidden(lambda a, b: [(PLANE_ONE[p + a - 1], y + b + 1) for p in (E1, O0, O1) for y in (1, 2)])
    two[0:3, 2:4] = value.reshape(3, 2, 64, 256)
    for load in loads[5:8]:
        load.wait()
    bias2 = jnp.transpose(jnp.broadcast_to(bias[1], (8, 256)))[:, :1]

    def clear_rows(planes):
        for there, r in ((has_up, 0), (has_down, 5)):
            pl.when(~there)(lambda r=r: clear(two, (planes, r)))

    def block(step, carry):
        @pl.when(step == 0)
        def _():
            arrived(*far)
            start(*far_outward, *far_inward)
            arrived(*near_inward, *far_inward)

        @pl.when(step == 1)
        def _():
            arrived(*near_outward)

        @pl.when(step == 2)
        def _():
            arrived(*far_outward, *far_seam)

        at_o1 = (2 - step) // 2
        rows = (-(step // 2), 3 + step // 2, step % 2 - 1, 4 - step % 2)

        def place(a, i):
            other = PLANE_ONE[(O0, E1)[i // 2] + a - 1]
            return other + at_o1 * (PLANE_ONE[O1 + a - 1] - other)

        value = hidden(lambda a, b: [(place(a, i), rows[i] + b + 1) for i in range(4)])
        for i in range(4):
            other = PLANE_TWO[(O0, E1)[i // 2]]
            two[other + at_o1 * (PLANE_TWO[O1] - other), rows[i] + 1] = value[i]

        @pl.when(step == 0)
        def _():
            clear_rows(2)
            start(plane_two)

        @pl.when(step == 1)
        def _():
            pl.when(~has_ext)(lambda: clear(two, (0,)))
            arrived(plane_two)
            pl.when((j == 0) | (j == CHAN - 1))(lambda: pl.semaphore_wait(relay, 1))

        @pl.when(step == 2)
        def _():
            pl.when(~has_ext)(lambda: clear(two, (0,)))
            clear_rows(slice(0, 2))

        pl.when(step > 0)(lambda: features(step - 1))
        return carry

    def features(n):
        pieces = lambda a, b: [(PLANE_TWO[p + a - 1], y + b) for p in (O0, O1) for y in (1 - n, 2 + n)]
        value = leaky(shifted_lanes(*accumulate(two, pieces, w2, True)) + bias2).astype(BF16)
        for q in range(2):
            p = q + flip * (1 - 2 * q)
            mine[n, :, pl.ds(pl.multiple_of(128 * p, 128), 128)] = value[:, 128 * q : 128 * q + 128]
        for k in range(2):
            pl.when(n == k)(lambda k=k: start(*turns[k]))
        pltpu.make_async_copy(mine.at[n, own_slab], got.at[n, j], local.at[10 + n]).start()

    lax.fori_loop(0, 3, block, 0)
    for n in range(2):
        pltpu.make_async_copy(mine.at[n, own_slab], got.at[n, j], local.at[10 + n]).wait()
        arrived(*turns[n])
    for copy, sends, _ in used:
        copy.wait_send() if sends is True else pl.when(sends)(copy.wait_send)


def regroup(got, out, built, sems):
    part, copies = SLAB // 2, []
    for k in range(2):
        channels = slice(part * k, part * k + part)
        for p in range(2):
            rows = [None] * 16
            for n in range(2):
                for source in range(CHAN):
                    pair = got[n, source, channels, 128 * p : 128 * p + 128].astype(F32)
                    rows[4 * source + 1 - n] = pair[:, :64]
                    rows[4 * source + 2 + n] = pair[:, 64:]
            built[channels, p] = pltpu.einshape("yoz->oyz", jnp.stack(rows, axis=0)).astype(BF16)
        copies.append(pltpu.make_async_copy(built.at[channels], out.at[channels], sems.at[k]))
        copies[k].start()
    for copy in copies:
        copy.wait()


def on_device(volume, first_filter, first_bias, second_filter, second_bias):
    voxels = jnp.transpose(volume, (1, 2, 3, 0))
    hbm, vmem = pl.BlockSpec(memory_space=pltpu.HBM), pl.BlockSpec(memory_space=pltpu.VMEM)
    dma = pltpu.SemaphoreType.DMA
    got = pl.pallas_call(
        kernel,
        out_shape=pltpu.VMEM((2, CHAN, SLAB, 256), BF16),
        in_specs=[hbm] * 5,
        out_specs=vmem,
        scratch_shapes=[
            pltpu.VMEM((5, 8, 64, 256), BF16),
            pltpu.VMEM((4, 6, 64, 256), BF16),
            pltpu.VMEM((27, 256, 256), BF16),
            pltpu.VMEM((27, 256, 256), BF16),
            pltpu.VMEM((2, 1, 256), F32),
            pltpu.VMEM((2, 256, 256), BF16),
            dma((12,)),
            dma((26,)),
            dma((26,)),
            pltpu.SemaphoreType.REGULAR,
        ],
        compiler_params=pltpu.CompilerParams(
            collective_id=0, has_side_effects=True, vmem_limit_bytes=62 * 2**20
        ),
        cost_estimate=pl.CostEstimate(flops=5_900_000_000, bytes_accessed=8_000_000, transcendentals=0),
    )(voxels, first_filter, first_bias.reshape(1, 256), second_filter, second_bias.reshape(1, 256))
    return pl.pallas_call(
        regroup,
        out_shape=jax.ShapeDtypeStruct((SLAB, 2, 16, 64), BF16),
        in_specs=[vmem],
        out_specs=hbm,
        scratch_shapes=[pltpu.VMEM((SLAB, 2, 16, 64), BF16), dma((2,))],
        compiler_params=pltpu.CompilerParams(vmem_limit_bytes=8 * 2**20),
        cost_estimate=pl.CostEstimate(flops=0, bytes_accessed=786432, transcendentals=0),
    )(got)


def solution(mesh):
    in_specs = (P(None, "space", "chan", None), P(), P(), P(), P())
    out_specs = P("chan", "space", None, None)
    return jax.shard_map(
        on_device, mesh=mesh, in_specs=in_specs, out_specs=out_specs, check_vma=False
    )
```

```python
import jax
import jax.numpy as jnp
from jax import lax
from jax.experimental import pallas as pl
from jax.experimental.pallas import tpu as pltpu
from jax.sharding import PartitionSpec as P

MESH = pl.DeviceIdType.MESH
F32, BF16 = jnp.float32, jnp.bfloat16
CHAN = 4
SLAB = 64
E2, E1, O0, O1, I1 = range(-2, 3)
PLANE_ONE = {E1: 0, E2: 1, O0: 2, O1: 3, I1: 4}
PLANE_TWO = {E1: 0, O0: 1, O1: 2, I1: 3}
OWN_ONE = slice(2, 6)


def leaky(value):
    return jnp.where(value >= 0.0, value, 0.3 * value)


def nt(a, b):
    return lax.dot_general(a, b, (((1,), (1,)), ((), ())), preferred_element_type=F32)


def shifted_rows(low, mid, high):
    rows = low.shape[0]
    z = lax.broadcasted_iota(jnp.int32, low.shape, 0) % 64
    up = jnp.where(z == 0, 0.0, pltpu.roll(low, 1, 0))
    down = jnp.where(z == 63, 0.0, pltpu.roll(high, rows - 1, 0))
    return mid + up + down


def shifted_lanes(low, mid, high):
    parts = []
    for first in range(0, low.shape[1], 128):
        cut = slice(first, first + 128)
        z = lax.broadcasted_iota(jnp.int32, (low.shape[0], 128), 1) % 64
        up = jnp.where(z == 0, 0.0, pltpu.roll(low[:, cut], 1, 1))
        down = jnp.where(z == 63, 0.0, pltpu.roll(high[:, cut], 127, 1))
        parts.append(mid[:, cut] + up + down)
    return jnp.concatenate(parts, axis=1)


def accumulate(block, pieces, filters, channels_first):
    sums = [None] * 3
    for a in range(3):
        for b in range(3):
            voxels = jnp.concatenate([block[place] for place in pieces(a, b)], axis=0)
            for c in range(3):
                taps = filters[9 * a + 3 * b + c]
                term = nt(taps, voxels) if channels_first else nt(voxels, taps)
                sums[c] = term if sums[c] is None else sums[c] + term
    return sums


def kernel(
    vol, f1, b1, f2, b2, got,
    one, two, w1, w2, bias, mine, local, send_sems, recv_sems, relay,
):
    s, j = lax.axis_index("space"), lax.axis_index("chan")
    flip = s % 2
    sib, ext = s + 1 - 2 * flip, s - 1 + 2 * flip
    has_ext = (ext >= 0) & (ext < lax.axis_size("space"))
    has_up, has_down = j > 0, j < CHAN - 1
    half = lax.axis_size("space") // 2
    seam = (s == half - 1) | (s == half)

    loads = [
        pltpu.make_async_copy(vol.at[flip], one.at[2, OWN_ONE], local.at[0]),
        pltpu.make_async_copy(vol.at[1 - flip], one.at[3, OWN_ONE], local.at[1]),
    ]
    for n, (src, dst) in enumerate(((f1, w1), (f2, w2))):
        for a in range(3):
            first = 9 * (a + flip * (2 - 2 * a))
            loads.append(pltpu.make_async_copy(src.at[pl.ds(first, 9)], dst.at[9 * a : 9 * a + 9], local.at[2 + 3 * n + a]))
    loads.append(pltpu.make_async_copy(b1, bias.at[0], local.at[8]))
    loads.append(pltpu.make_async_copy(b2, bias.at[1], local.at[9]))
    for load in loads[:2]:
        load.start()

    barrier = pltpu.get_barrier_semaphore()
    pl.semaphore_signal(barrier, inc=1, device_id=(sib, j), device_id_type=MESH)
    greeted = ((has_ext, (ext, j)), (has_up, (s, j - 1)), (has_down, (s, j + 1)))
    for there, who in greeted:
        @pl.when(there)
        def _(who=who):
            pl.semaphore_signal(barrier, inc=1, device_id=who, device_id_type=MESH)
    for load in loads[2:]:
        load.start()

    def clear(ref, place):
        ref[place] = jnp.zeros(ref.at[place].shape, BF16)

    pl.when(~has_ext)(lambda: clear(one, (slice(0, 2),)))
    for there, places in ((has_up, (0, 1)), (has_down, (6, 7))):
        for place in places:
            pl.when(~there)(lambda place=place: clear(one, (slice(None), place)))

    used = []

    def remote(src, dst, to, sends, receives):
        n = len(used)
        copy = pltpu.make_async_remote_copy(
            src_ref=src, dst_ref=dst, send_sem=send_sems.at[n], recv_sem=recv_sems.at[n],
            device_id=to, device_id_type=MESH,
        )
        used.append((copy, sends, receives))
        return used[-1]

    def start(*copies):
        for copy, sends, _ in copies:
            copy.start() if sends is True else pl.when(sends)(copy.start)

    def arrived(*copies):
        for copy, _, receives in copies:
            copy.wait_recv() if receives is True else pl.when(receives)(copy.wait_recv)

    sibling, outside, above, below = (sib, j), (ext, j), (s, j - 1), (s, j + 1)
    to_sib = remote(one.at[3, OWN_ONE], one.at[4, OWN_ONE], sibling, True, True)
    to_ext = remote(one.at[2:4, OWN_ONE], one.at[0:2, OWN_ONE], outside, has_ext, has_ext)
    near = (
        remote(one.at[2:4, 2], one.at[2:4, 6], above, has_up, has_down),
        remote(one.at[2:4, 5], one.at[2:4, 1], below, has_down, has_up),
    )
    far = (
        remote(one.at[2:4, 3], one.at[2:4, 7], above, has_up, has_down),
        remote(one.at[2:4, 4], one.at[2:4, 0], below, has_down, has_up),
    )
    far_seam = (
        remote(one.at[0:2, 3], one.at[0:2, 7], above, seam & has_up, seam & has_down),
        remote(one.at[0:2, 4], one.at[0:2, 0], below, seam & has_down, seam & has_up),
    )

    def corners(r_up, r_down, outer):
        outward, inward = [], []
        for r, there in ((r_up, has_up), (r_down, has_down)):
            passed = outer & there
            outward.append(remote(one.at[2:4, r], one.at[0:2, r], outside, passed, passed))
            inward.append(remote(one.at[3, r], one.at[4, r], sibling, there, there))
        return outward, inward

    near_outward, near_inward = corners(1, 6, has_ext)
    far_outward, far_inward = corners(0, 7, has_ext & ~seam)
    plane_two = remote(two.at[2], two.at[3], sibling, True, True)
    own_slab = pl.ds(pl.multiple_of(j * SLAB, SLAB), SLAB)
    turns = []
    for n in range(2):
        turns.append([])
        for step in (2, 1, 3):
            to = (j + step) % CHAN
            turns[n].append(remote(
                mine.at[n, pl.ds(pl.multiple_of(to * SLAB, SLAB), SLAB)], got.at[n, j], (s, to), True, True
            ))

    loads[0].wait()
    loads[1].wait()
    pl.semaphore_wait(barrier, 1 + sum(there.astype(jnp.int32) for there, _ in greeted))
    pl.when(seam)(to_ext[0].start)
    start(*near)
    pl.when(has_ext & ~seam)(to_ext[0].start)
    busy = ((s + 2) % half < 4) & ~seam
    start(to_sib)
    for copy, sends, _ in far:
        pl.when(sends & ~busy)(copy.start)

    arrived(*near)
    start(*near_outward, *near_inward)
    for copy, sends, _ in far:
        pl.when(sends & busy)(copy.start)
    for at, tell in ((1, 0), (2, 3)):
        @pl.when(j == at)
        def _(tell=tell):
            pl.semaphore_signal(relay, inc=1, device_id=(s, tell), device_id_type=MESH)
    for load in loads[2:5] + loads[8:]:
        load.wait()
    bias1 = bias[0]
    arrived(to_ext)
    start(*far_seam)
    arrived(to_sib)

    def hidden(pieces):
        return leaky(shifted_rows(*accumulate(one, pieces, w1, False)) + bias1).astype(BF16).reshape(-1, 64, 256)

    value = hidden(lambda a, b: [(PLANE_ONE[p + a - 1], y + b + 1) for p in (E1, O0, O1) for y in (1, 2)])
    two[0:3, 2:4] = value.reshape(3, 2, 64, 256)
    for load in loads[5:8]:
        load.wait()
    bias2 = jnp.transpose(jnp.broadcast_to(bias[1], (8, 256)))[:, :1]

    def clear_rows(planes):
        for there, r in ((has_up, 0), (has_down, 5)):
            pl.when(~there)(lambda r=r: clear(two, (planes, r)))

    def block(step, carry):
        @pl.when(step == 0)
        def _():
            arrived(*far)
            start(*far_outward, *far_inward)
            arrived(*near_inward, *far_inward)

        @pl.when(step == 1)
        def _():
            arrived(*near_outward)

        @pl.when(step == 2)
        def _():
            arrived(*far_outward, *far_seam)

        at_o1 = (2 - step) // 2
        rows = (-(step // 2), 3 + step // 2, step % 2 - 1, 4 - step % 2)

        def place(a, i):
            other = PLANE_ONE[(O0, E1)[i // 2] + a - 1]
            return other + at_o1 * (PLANE_ONE[O1 + a - 1] - other)

        value = hidden(lambda a, b: [(place(a, i), rows[i] + b + 1) for i in range(4)])
        for i in range(4):
            other = PLANE_TWO[(O0, E1)[i // 2]]
            two[other + at_o1 * (PLANE_TWO[O1] - other), rows[i] + 1] = value[i]

        @pl.when(step == 0)
        def _():
            clear_rows(2)
            start(plane_two)

        @pl.when(step == 1)
        def _():
            pl.when(~has_ext)(lambda: clear(two, (0,)))
            arrived(plane_two)
            pl.when((j == 0) | (j == CHAN - 1))(lambda: pl.semaphore_wait(relay, 1))

        @pl.when(step == 2)
        def _():
            pl.when(~has_ext)(lambda: clear(two, (0,)))
            clear_rows(slice(0, 2))

        pl.when(step > 0)(lambda: features(step - 1))
        return carry

    def features(n):
        pieces = lambda a, b: [(PLANE_TWO[p + a - 1], y + b) for p in (O0, O1) for y in (1 - n, 2 + n)]
        value = leaky(shifted_lanes(*accumulate(two, pieces, w2, True)) + bias2).astype(BF16)
        for q in range(2):
            p = q + flip * (1 - 2 * q)
            mine[n, :, pl.ds(pl.multiple_of(128 * p, 128), 128)] = value[:, 128 * q : 128 * q + 128]
        for k in range(2):
            pl.when(n == k)(lambda k=k: start(*turns[k]))
        pltpu.make_async_copy(mine.at[n, own_slab], got.at[n, j], local.at[10 + n]).start()

    lax.fori_loop(0, 3, block, 0)
    for n in range(2):
        pltpu.make_async_copy(mine.at[n, own_slab], got.at[n, j], local.at[10 + n]).wait()
        arrived(*turns[n])
    for copy, sends, _ in used:
        copy.wait_send() if sends is True else pl.when(sends)(copy.wait_send)


def regroup(got, out, built, sems):
    part, copies = SLAB // 2, []
    for k in range(2):
        channels = slice(part * k, part * k + part)
        for p in range(2):
            rows = [None] * 16
            for n in range(2):
                for source in range(CHAN):
                    pair = got[n, source, channels, 128 * p : 128 * p + 128].astype(F32)
                    rows[4 * source + 1 - n] = pair[:, :64]
                    rows[4 * source + 2 + n] = pair[:, 64:]
            built[channels, p] = pltpu.einshape("yoz->oyz", jnp.stack(rows, axis=0)).astype(BF16)
            copies.append(pltpu.make_async_copy(built.at[channels, p], out.at[channels, p], sems.at[2 * k + p]))
            copies[-1].start()
    for copy in copies:
        copy.wait()


def on_device(volume, first_filter, first_bias, second_filter, second_bias):
    voxels = jnp.transpose(volume, (1, 2, 3, 0))
    hbm, vmem = pl.BlockSpec(memory_space=pltpu.HBM), pl.BlockSpec(memory_space=pltpu.VMEM)
    dma = pltpu.SemaphoreType.DMA
    got = pl.pallas_call(
        kernel,
        out_shape=pltpu.VMEM((2, CHAN, SLAB, 256), BF16),
        in_specs=[hbm] * 5,
        out_specs=vmem,
        scratch_shapes=[
            pltpu.VMEM((5, 8, 64, 256), BF16),
            pltpu.VMEM((4, 6, 64, 256), BF16),
            pltpu.VMEM((27, 256, 256), BF16),
            pltpu.VMEM((27, 256, 256), BF16),
            pltpu.VMEM((2, 1, 256), F32),
            pltpu.VMEM((2, 256, 256), BF16),
            dma((12,)),
            dma((26,)),
            dma((26,)),
            pltpu.SemaphoreType.REGULAR,
        ],
        compiler_params=pltpu.CompilerParams(
            collective_id=0, has_side_effects=True, vmem_limit_bytes=62 * 2**20
        ),
        cost_estimate=pl.CostEstimate(flops=5_900_000_000, bytes_accessed=8_000_000, transcendentals=0),
    )(voxels, first_filter, first_bias.reshape(1, 256), second_filter, second_bias.reshape(1, 256))
    return pl.pallas_call(
        regroup,
        out_shape=jax.ShapeDtypeStruct((SLAB, 2, 16, 64), BF16),
        in_specs=[vmem],
        out_specs=hbm,
        scratch_shapes=[pltpu.VMEM((SLAB, 2, 16, 64), BF16), dma((4,))],
        compiler_params=pltpu.CompilerParams(vmem_limit_bytes=8 * 2**20),
        cost_estimate=pl.CostEstimate(flops=0, bytes_accessed=786432, transcendentals=0),
    )(got)


def solution(mesh):
    in_specs = (P(None, "space", "chan", None), P(), P(), P(), P())
    out_specs = P("chan", "space", None, None)
    return jax.shard_map(
        on_device, mesh=mesh, in_specs=in_specs, out_specs=out_specs, check_vma=False
    )
```
